512 devices in a mesh: dp: 128 (over z, y, core), grp: 4 (over x).
Axes of the slice: x: 4, y: 4, z: 16, core: 2. Of those that a mesh axis runs over, the one named last changes fastest.
Arguments:
- embeddings: bfloat16 [131072, 1024], P(('dp', 'grp')), may hold values from -24 to 24
- coarse_ids: int32 [131072, 1], P(('dp', 'grp')), may hold values from 0 to 255; in each aligned block of 256 rows (0 to 255, 256 to 511, ...) at most 2 rows name the same one
- owner_slot: int32 [256], replicated, may hold values from 0 to 255, each once
- coarse_centroids: bfloat16 [256, 1024], replicated, may hold values from -6 to 7
- child_centroids: bfloat16 [256, 400, 1024], P('dp'), may hold values from -6 to 7
Outputs:
- new_coarse: float32 [256, 1024], replicated
- new_children: float32 [256, 400, 1024], P('dp', 'grp')
The draws below stay inside these ranges and needn't reach their ends.
Inputs may be any that keep to these rules, and one draw needn't show every extreme that they name: `coarse_ids`: within the rows of one device no coarse cluster appears more than 2 times, and some cluster appears exactly 2 times in every draw. `owner_slot`: a permutation; the children of coarse cluster c are child_centroids[owner_slot[c]].
All inputs are finite; a program needn't handle non-finite values.
Results may differ from the reference program's by a relative error of at most 0.0004.
Values may be sent and summed in bfloat16 or wider, within the bound.
A program may use at most 64 MiB of HBM per device.

```python
import math
import jax
import jax.numpy as jnp
import numpy as np
from jax import lax

D = 1024
NCOARSE = 256
CHILD = 400
ROWS_DEV = 256
CAPACITY = 2
TOKENS = 131072
N_DP = 128
N_GRP = 4


def draw_coarse_centroids(key, part):
    key = jax.random.fold_in(key, 11)
    base_key = jax.random.fold_in(key, 0)
    values = jnp.clip(jax.random.normal(base_key, (NCOARSE, D), jnp.float32), -6.0, 6.0)
    return values.astype(jnp.bfloat16)


def draw_child_centroids(key, part):
    key = jax.random.fold_in(key, 23)
    base_key = jax.random.fold_in(key, 0)
    values = jnp.clip(jax.random.normal(base_key, (NCOARSE, CHILD, D), jnp.float32), -6.0, 6.0)
    return values.astype(jnp.bfloat16)


def strengthened(result, key, source, target, blocks, factor):
    def block_of(position):
        return (jnp.arange(result.shape[position]) // (result.shape[position] // blocks)).reshape((-1,) + (1,) * (result.ndim - 1 - position))

    near = jax.random.permutation(key, blocks)[block_of(target)]
    far = (block_of(target) + blocks // 2) % blocks
    return jnp.where((block_of(source) == near) | (block_of(source) == far), factor * result, result)


def levels(rng, shape, shards, least, high):
    level, own = 1.0, jax.random.fold_in(rng, 6)
    for dim, parts in shards:
        steps = jnp.exp(jax.random.uniform(jax.random.fold_in(own, dim), (parts,), jnp.float32, least / len(shards), high / len(shards)))
        level = level * jnp.repeat(steps, shape[dim] // parts).reshape([-1 if axis == dim else 1 for axis in range(len(shape))])
    return level


def shared_out(stream_key, own, number, rows, amount, top, limit, slope):
    order = jax.random.permutation(stream_key, amount)
    heavy_load, usual = portions_of(amount, rows * top, limit, slope, True), portions_of(amount, rows * top, limit, slope, False)
    places = jnp.arange(amount)

    def named(sizes, offset_by):
        used = int((sizes > 0).sum())
        fixed = max(1, used // 4)
        shifted = fixed + (places - fixed + offset_by * (used - fixed)) % max(1, amount - fixed)
        return jnp.zeros((amount,), jnp.int32).at[order[jnp.where(places < fixed, places, shifted)]].set(jnp.asarray(sizes, jnp.int32))

    sizes = jnp.where(number % 4 == 0, named(heavy_load, number // 4), named(usual, number - number // 4 - 1))
    mixed = jax.random.permutation(jax.random.fold_in(own, 3), amount)
    donor, receiver = mixed[0:amount // 2 * 2:2], mixed[1:amount // 2 * 2:2]
    margin = jnp.minimum(sizes[donor] - 1, limit - sizes[receiver]) // 2
    margin = jnp.where((donor == order[0]) | (receiver == order[0]) | (sizes[receiver] == 0), 0, jnp.maximum(margin, 0))
    shifted = jax.random.randint(jax.random.fold_in(own, 4), (amount // 2,), 0, 1 << 20) % (margin + 1)
    sizes = sizes.at[donor].add(-shifted).at[receiver].add(shifted)
    items = jnp.searchsorted(jnp.cumsum(sizes), jnp.arange(rows * top), side="right").astype(jnp.int32)
    listing = items.reshape(top, rows).T
    listing = listing[jax.random.permutation(jax.random.fold_in(own, 1), rows)]
    offset_by = jax.random.randint(jax.random.fold_in(own, 2), (rows, 1), 0, top)
    return jnp.take_along_axis(listing, (jnp.arange(top)[None, :] + offset_by) % top, axis=1)


def portions_of(amount, total, limit, slope, full):
    loads = [(1 << 20) // math.isqrt(standing ** slope) + 1 for standing in range(1, amount + 1)]
    largest = limit if full else min(limit, max(-(-total // amount), total * loads[0] // sum(loads)))
    least = 1 if total - largest >= amount - 1 else 0
    holding, spare = [largest] + [least] * (amount - 1), total - largest - least * (amount - 1)
    while spare > 0:
        free = [i for i in range(1, amount) if holding[i] < largest] or [i for i in range(1, amount) if holding[i] < limit]
        whole, remaining = sum([loads[i] for i in free]), spare
        for i in free:
            extra = min(limit - holding[i], max(1, remaining * loads[i] // whole), spare)
            holding[i] = holding[i] + extra
            spare = spare - extra
    return np.array(holding)


def gaussian_with(key, dims, scale, limit, cuts, heavy, held_as=jnp.bfloat16):
    array = scale * jax.random.normal(key, dims, jnp.float32)
    if cuts:
        array = array * levels(key, dims, cuts, -0.22, 0.18)
    return jnp.clip(strengthened(array, jax.random.fold_in(key, 3), *heavy), -limit, limit).astype(held_as)


def setup_inputs(seed: int = 0) -> dict:
    seeds = jax.random.split(jax.random.key(seed), 6)
    embeddings = gaussian_with(seeds[0], (TOKENS, D), 1.0, 24.0, ((0, 512),), (0, 1, 512, 6.0))
    coarse_ids_keys = jax.random.split(jax.random.fold_in(seeds[1], 1), TOKENS // ROWS_DEV)
    coarse_ids_turns = jax.random.permutation(jax.random.fold_in(seeds[1], 3), TOKENS // ROWS_DEV)
    coarse_ids = jax.vmap(lambda own, number: shared_out(jax.random.fold_in(seeds[1], 2), own, number, ROWS_DEV, NCOARSE, 1, CAPACITY, 2))(coarse_ids_keys, coarse_ids_turns).reshape((TOKENS, 1))
    owner_slot = jax.random.permutation(seeds[2], NCOARSE).astype(jnp.int32)
    coarse_centroids = draw_coarse_centroids(jax.random.fold_in(seeds[5], 71), 0)
    child_centroids = draw_child_centroids(jax.random.fold_in(seeds[5], 71), 0)
    return {"embeddings": embeddings, "coarse_ids": coarse_ids, "owner_slot": owner_slot, "coarse_centroids": coarse_centroids, "child_centroids": child_centroids}


prior_weight = 1.0


def soft_weights(scores):
    highest = jnp.max(scores, axis=-1, keepdims=True)
    raised = jnp.exp(scores - highest)
    return (raised / jnp.sum(raised, axis=-1, keepdims=True)).astype(jnp.bfloat16)


def reference(embeddings, coarse_ids, owner_slot, coarse_centroids, child_centroids):
    scale = D ** -0.5
    coarse_norms = jnp.sum(coarse_centroids.astype(jnp.float32) ** 2, axis=1)
    blocks = embeddings.reshape(TOKENS // ROWS_DEV, ROWS_DEV, D)

    def coarse_step(carry, block):
        products = jnp.dot(block, coarse_centroids.T, preferred_element_type=jnp.float32)
        weights = soft_weights((products - 0.5 * coarse_norms[None, :]) * scale)
        sums = carry[0] + jnp.dot(weights.T, block, preferred_element_type=jnp.float32)
        masses = carry[1] + jnp.sum(weights.astype(jnp.float32), axis=0)
        return (sums, masses), None

    start_carry = (jnp.zeros((NCOARSE, D), jnp.float32), jnp.zeros((NCOARSE,), jnp.float32))
    (coarse_sums, coarse_mass), _ = lax.scan(coarse_step, start_carry, blocks)
    new_coarse = (coarse_sums + prior_weight * coarse_centroids.astype(jnp.float32)) / (coarse_mass + prior_weight)[:, None]

    placed = owner_slot[coarse_ids[:, 0]].astype(jnp.int32)
    order = jnp.argsort(placed, stable=True).astype(jnp.int32)
    counts = jax.ops.segment_sum(jnp.ones((TOKENS,), jnp.int32), placed, num_segments=NCOARSE)
    starts = jnp.cumsum(counts) - counts
    most_rows = N_DP * N_GRP * max(2, ROWS_DEV // 128)
    offsets = jnp.arange(most_rows, dtype=jnp.int32)

    def per_slot(index):
        picks = jnp.minimum(starts[index] + offsets, TOKENS - 1).astype(jnp.int32)
        valid = (offsets < counts[index]).astype(jnp.bfloat16)
        block = embeddings[order[picks]]
        centers = child_centroids[index]
        norms = jnp.sum(centers.astype(jnp.float32) ** 2, axis=1)
        products = jnp.dot(block, centers.T, preferred_element_type=jnp.float32)
        weights = soft_weights((products - 0.5 * norms[None, :]) * scale) * valid[:, None]
        sums = jnp.dot(weights.T, block, preferred_element_type=jnp.float32)
        masses = jnp.sum(weights.astype(jnp.float32), axis=0)
        return sums, masses

    child_sums, child_mass = lax.map(per_slot, jnp.arange(NCOARSE, dtype=jnp.int32))
    new_children = (child_sums + prior_weight * child_centroids.astype(jnp.float32)) / (child_mass + prior_weight)[:, :, None]
    return new_coarse, new_children
```

```python
import functools

import jax
import jax.numpy as jnp
from jax import lax
from jax.experimental import pallas as pl
from jax.experimental.pallas import tpu as pltpu
from jax.sharding import PartitionSpec as P

MESH = pl.DeviceIdType.MESH
prior_weight = 1.0
NZ, NP, NX = 16, 8, 4
MARK = 2.0**100
DISTANCE = [[7, 9, 8, 0], [5, 11, 6, 10], [3, 13, 4, 12], [1, 15, 2, 14]]
FLAT = [d for part in DISTANCE for d in part]


def iota(shape, dim):
    return lax.broadcasted_iota(jnp.int32, shape, dim)


def dot(a, b):
    return jnp.dot(a, b, preferred_element_type=jnp.float32)


def dot_t(a, b):
    return lax.dot_general(a, b, (((1,), (1,)), ((), ())), preferred_element_type=jnp.float32)


def column_softmax(scores):
    raised = jnp.exp(scores - jnp.max(scores, axis=0, keepdims=True))
    return raised * (1.0 / jnp.sum(raised, axis=0, keepdims=True))


def kernel(
    ids_ref, slot_ref, emb_ref, cc_ref, cent_hbm,
    coarse_out, child_out,
    cent, norms, acc, mass, out_a, in_a, zs, rows,
    csend, crecv, xsend, xrecv, zbuf, zrecv,
    cent_sem, a_send, a_recv, z_send, z_recv, x_send, x_recv, r_send, r_recv,
    c_send, c_recv, cx_send, cx_recv, cz_send, cz_recv, gx_send, gx_recv, gp_send, gp_recv,
):
    dp = lax.axis_index("dp")
    x = lax.axis_index("grp")
    z, p = dp // NP, dp % NP
    count, width = emb_ref.shape
    nchild = cent_hbm.shape[1]
    share = child_out.shape[1]
    scale = width ** (-0.5)

    def at_p(k):
        return (z * NP + (p + k) % NP, x)

    def at_z(d):
        return (((z + d) % NZ) * NP + p, x)

    def at_x(k):
        return (dp, (x + k) % NX)

    barrier = pltpu.get_barrier_semaphore()
    for k in range(1, NP):
        pl.semaphore_signal(barrier, inc=1, device_id=at_p(k), device_id_type=MESH)
    for k in range(1, NX):
        pl.semaphore_signal(barrier, inc=1, device_id=at_x(k), device_id_type=MESH)
    for k in range(1, NZ):
        pl.semaphore_signal(barrier, inc=1, device_id=at_z(k), device_id_type=MESH)
    cent_copy = pltpu.make_async_copy(cent_hbm, cent.at[:, pl.ds(0, nchild)], cent_sem)
    cent_copy.start()

    pending = []

    def send(src, dst, send_sem, recv_sem, device):
        copy = pltpu.make_async_remote_copy(
            src_ref=src, dst_ref=dst, send_sem=send_sem, recv_sem=recv_sem,
            device_id=device, device_id_type=MESH,
        )
        copy.start()
        pending.append(copy)

    def arrived(dst, sem):
        pltpu.make_async_remote_copy(
            src_ref=dst, dst_ref=dst, send_sem=sem, recv_sem=sem,
            device_id=at_x(1), device_id_type=MESH,
        ).wait_recv()

    square = (count, count)
    diagonal = iota(square, 0) == iota(square, 1)
    ids_row = ids_ref[...]
    ids_col = jnp.sum(jnp.where(diagonal, ids_row, 0), axis=1, keepdims=True)
    slot_col = jnp.sum(jnp.where(diagonal, slot_ref[...], 0), axis=1, keepdims=True)
    placed = jnp.sum(jnp.where(ids_row == iota(square, 0), slot_col, 0), axis=0, keepdims=True)
    before = (ids_col == ids_row) & (iota(square, 0) < iota(square, 1))
    position = jnp.sum(before.astype(jnp.int32), axis=0, keepdims=True)
    target = placed * 2 + position

    emb = emb_ref[...]
    for j in range(4):
        r = iota((NP * 16, 1), 0)
        peer, q, low = r // 16, (r // 4) % 4, r % 4
        d0, d1, d2, d3 = DISTANCE[j]
        distance = jnp.where(q == 0, d0, jnp.where(q == 1, d1, jnp.where(q == 2, d2, d3)))
        key = ((z + distance) % NZ) * (NP * 4) + peer * 4 + low
        pick = (key == target).astype(jnp.float32)
        empty = jnp.sum(pick, axis=1, keepdims=True) < 0.5
        block = dot(pick.astype(jnp.bfloat16), emb)
        block = jnp.where(empty & (iota((1, width), 1) == 0), MARK, block)
        out_a[j] = block.astype(jnp.bfloat16).reshape(NP, 16, width)

    pl.semaphore_wait(barrier, NP - 1 + NX - 1 + NZ - 1)

    for j in range(4):
        for k in range(1, NP):
            send(out_a.at[j, (p + k) % NP], in_a.at[j, p], a_send.at[j, k], a_recv.at[j, k], at_p(k))
        in_a[j, p] = out_a[j, p]

    cc = cc_ref[...]
    cc32 = cc.astype(jnp.float32)
    coarse_norms = jnp.sum(cc32 * cc32, axis=1, keepdims=True)
    weights = column_softmax((dot_t(cc, emb) - 0.5 * coarse_norms) * scale).astype(jnp.bfloat16)
    csend[:, :, :width] = dot(weights, emb).reshape(NP, 32, width)
    coarse_mass = jnp.sum(weights.astype(jnp.float32), axis=1, keepdims=True)
    csend[:, :, width:] = jnp.broadcast_to(coarse_mass, (count, 128)).reshape(NP, 32, 128)
    for k in range(1, NP):
        send(csend.at[(p + k) % NP], crecv.at[k], c_send.at[k], c_recv.at[k], at_p(k))

    o, i = iota((128, 128), 0), iota((128, 128), 1)
    source = ((o // 2) % 8) * 16 + (o // 32) * 4 + ((o // 16) % 2) * 2 + o % 2
    reorder = (i == source).astype(jnp.bfloat16)
    for j in range(4):
        for k in range(1, NP):
            arrived(in_a.at[j, (p - k + NP) % NP], a_recv.at[j, k])
        blocks = dot(reorder, in_a[j].reshape(128, width)).astype(jnp.bfloat16)
        blocks = blocks.reshape(4, 2, 16, width)
        zs[pl.ds(4 * j, 4)] = blocks
        for q in range(4):
            d, n = DISTANCE[j][q], 4 * j + q
            if d == 0:
                rows[0, n] = blocks[q]
            else:
                send(zs.at[n], rows.at[0, n], z_send.at[n], z_recv.at[n], at_z(d))

    cent_copy.wait()
    first = (iota((16, width), 0) == 0) & (iota((16, width), 1) == 0)
    for b in range(2):
        c32 = cent[b, :nchild].astype(jnp.float32)
        norms[b] = jnp.sum(c32 * c32, axis=1, keepdims=True)
        cent[b, nchild:] = first.astype(jnp.bfloat16)
    acc[...] = jnp.zeros_like(acc)
    mass[...] = jnp.zeros_like(mass)
    mine = (iota((128, nchild), 1) == iota((128, nchild), 0) + x * share) & (iota((128, nchild), 0) < share)
    mine = mine.astype(jnp.bfloat16)

    def score(j):
        def one(b, carry):
            block = rows[:, pl.ds(4 * j, 4), b].reshape(256, width)
            products = dot_t(cent[b], block)
            weights = column_softmax((products[:nchild] - 0.5 * norms[b]) * scale)
            weights = jnp.where(products[nchild : nchild + 1] < 0.5 * MARK, weights, 0.0)
            own = dot(mine, weights.astype(jnp.bfloat16))
            mass[b] += jnp.sum(own, axis=1, keepdims=True)
            acc[b] += dot(own.astype(jnp.bfloat16), block)
            return carry

        lax.fori_loop(0, 2, one, 0)

    def pass_on(n):
        if FLAT[n] != 0:
            arrived(rows.at[0, n], z_recv.at[n])
        send(rows.at[0, n], rows.at[1, n], x_send.at[n, 0], x_recv.at[n, 0], at_x(1))
        send(rows.at[0, n], rows.at[3, n], x_send.at[n, 1], x_recv.at[n, 1], at_x(3))

    def relay(n):
        arrived(rows.at[1, n], x_recv.at[n, 0])
        send(rows.at[1, n, 0], rows.at[2, n, 0], r_send.at[n, 0], r_recv.at[n, 0], at_x(1))
        arrived(rows.at[3, n], x_recv.at[n, 1])
        send(rows.at[3, n, 1], rows.at[2, n, 1], r_send.at[n, 1], r_recv.at[n, 1], at_x(3))

    def landed(n):
        arrived(rows.at[2, n, 0], r_recv.at[n, 0])
        arrived(rows.at[2, n, 1], r_recv.at[n, 1])

    def coarse_step(s):
        if s == 0:
            total = csend[p]
            for k in range(1, NP):
                arrived(crecv.at[k], c_recv.at[k])
                total = total + crecv[k]
            xsend[...] = total.reshape(NX, 8, width + 128)
            for k in range(1, NX):
                send(xsend.at[(x + k) % NX], xrecv.at[k], cx_send.at[k], cx_recv.at[k], at_x(k))
        elif s == 1:
            total = xsend[x]
            for k in range(1, NX):
                arrived(xrecv.at[k], cx_recv.at[k])
                total = total + xrecv[k]
            zbuf[0] = total
        if 1 <= s <= 5:
            if s > 1:
                arrived(zrecv.at[s - 2], cz_recv.at[s - 2])
                zbuf[s - 1] = zbuf[s - 2] + zrecv[s - 2]
            if s < 5:
                d = 1 << (s - 1)
                partner = z + d * (1 - 2 * ((z // d) % 2))
                send(
                    zbuf.at[s - 1], zrecv.at[s - 1], cz_send.at[s - 1], cz_recv.at[s - 1],
                    (partner * NP + p, x),
                )
            else:
                own = (iota((8, count), 1) == p * 32 + x * 8 + iota((8, count), 0)).astype(jnp.bfloat16)
                centers = dot(own, cc_ref[...])
                coarse_out[p, x] = (zbuf[4, :, :width] + prior_weight * centers) / (
                    zbuf[4, :, width : width + 1] + prior_weight
                )
                for k in range(1, NX):
                    send(coarse_out.at[p, x], coarse_out.at[p, x], gx_send.at[k], gx_recv.at[k], at_x(k))
        if s == 6:
            for k in range(1, NX):
                arrived(coarse_out.at[p, (x - k + NX) % NX], gx_recv.at[k])
            for k in range(1, NP):
                send(coarse_out.at[p], coarse_out.at[p], gp_send.at[k], gp_recv.at[k], at_p(k))
        if s == 7:
            for k in range(1, NP):
                arrived(coarse_out.at[(p - k + NP) % NP], gp_recv.at[k])

    steps = {3: 0, 5: 1, 6: 2, 7: 3, 8: 4, 9: 5, 11: 6}
    for n in range(NZ + 2):
        if n < NZ:
            pass_on(n)
        if 1 <= n <= NZ:
            relay(n - 1)
        if n >= 2:
            landed(n - 2)
            if (n - 2) % 4 == 3:
                score((n - 2) // 4)
        if n in steps:
            coarse_step(steps[n])
    centers = [dot(mine, cent[b, :nchild]) for b in range(2)]
    for b in range(2):
        value = (acc[b] + prior_weight * centers[b]) / (mass[b] + prior_weight)
        child_out[b] = value[:share]
    coarse_step(7)
    for copy in pending:
        copy.wait_send()


def on_device(embeddings, coarse_ids, owner_slot, coarse_centroids, child_centroids):
    count, width = embeddings.shape
    _, nchild, _ = child_centroids.shape
    share = nchild // NX
    f32, bf16 = jnp.float32, jnp.bfloat16
    vmem = pl.BlockSpec(memory_space=pltpu.VMEM)
    dma = pltpu.SemaphoreType.DMA
    coarse, children = pl.pallas_call(
        kernel,
        out_shape=(
            jax.ShapeDtypeStruct((NP, NX, 8, width), f32),
            jax.ShapeDtypeStruct((2, share, width), f32),
        ),
        in_specs=[vmem, vmem, vmem, vmem, pl.BlockSpec(memory_space=pl.ANY)],
        out_specs=(vmem, vmem),
        scratch_shapes=[
            pltpu.VMEM((2, nchild + 16, width), bf16),
            pltpu.VMEM((2, nchild, 1), f32),
            pltpu.VMEM((2, 128, width), f32),
            pltpu.VMEM((2, 128, 1), f32),
            pltpu.VMEM((4, NP, 16, width), bf16),
            pltpu.VMEM((4, NP, 16, width), bf16),
            pltpu.VMEM((NZ, 2, 16, width), bf16),
            pltpu.VMEM((NX, NZ, 2, 16, width), bf16),
            pltpu.VMEM((NP, 32, width + 128), f32),
            pltpu.VMEM((NP, 32, width + 128), f32),
            pltpu.VMEM((NX, 8, width + 128), f32),
            pltpu.VMEM((NX, 8, width + 128), f32),
            pltpu.VMEM((5, 8, width + 128), f32),
            pltpu.VMEM((4, 8, width + 128), f32),
            dma,
            dma((4, NP)), dma((4, NP)),
            dma((NZ,)), dma((NZ,)),
            dma((NZ, 2)), dma((NZ, 2)),
            dma((NZ, 2)), dma((NZ, 2)),
            dma((NP,)), dma((NP,)),
            dma((NX,)), dma((NX,)),
            dma((4,)), dma((4,)),
            dma((NX,)), dma((NX,)),
            dma((NP,)), dma((NP,)),
        ],
        compiler_params=pltpu.CompilerParams(
            collective_id=0, has_side_effects=True, vmem_limit_bytes=48 * 1024 * 1024
        ),
    )(
        coarse_ids.reshape(1, count),
        owner_slot.reshape(1, -1),
        embeddings,
        coarse_centroids,
        child_centroids,
    )
    return coarse.reshape(coarse_centroids.shape), children


def solution(mesh):
    return jax.shard_map(
        on_device,
        mesh=mesh,
        in_specs=(P(("dp", "grp"), None), P(("dp", "grp"), None), P(), P(), P("dp", None, None)),
        out_specs=(P(), P("dp", "grp", None)),
        check_vma=False,
    )
```

```python
import jax
import jax.numpy as jnp
from jax import lax
from jax.experimental import pallas as pl
from jax.experimental.pallas import tpu as pltpu
from jax.sharding import PartitionSpec as P

MESH = pl.DeviceIdType.MESH
prior_weight = 1.0
NZ, NY, NC, NX = 16, 4, 2, 4
NP = NY * NC
MARK = 2.0**100
DISTANCE = (0, 1, 15, 2, 14, 3, 13, 4, 12, 5, 11, 6, 10, 7, 9, 8)
AHEAD = (8, 9, 10, 11, 12, 13, 14, 15, 15, 15, 15, 15, 15, 15, 15, 15)


def iota(shape, dim):
    return lax.broadcasted_iota(jnp.int32, shape, dim)


def dot(a, b):
    return jnp.dot(a, b, preferred_element_type=jnp.float32)


def dot_t(a, b):
    return lax.dot_general(a, b, (((1,), (1,)), ((), ())), preferred_element_type=jnp.float32)


def column_softmax(scores):
    raised = jnp.exp(scores - jnp.max(scores, axis=0, keepdims=True))
    return raised * (1.0 / jnp.sum(raised, axis=0, keepdims=True))


def kernel(
    ids_hbm, slot_hbm, emb_hbm, cc_hbm, cent_hbm,
    coarse_out, child_out,
    ids_ref, slot_ref, emb_ref, cc_ref, cent, norms, acc, mass, out_a, in_a, zs, rows,
    cbuf, crecv, ybuf, yrecv, xbuf, xrecv, zbuf, zrecv, tiles, centers8,
    load_sem, a_send, a_recv, z_send, z_recv, x_send, x_recv, r_send, r_recv,
    c_send, c_recv, cy_send, cy_recv, cx_send, cx_recv, cz_send, cz_recv,
    gz_send, gz_recv, gx_send, gx_recv, gy_send, gy_recv, gc_send, gc_recv,
):
    dp = lax.axis_index("dp")
    x = lax.axis_index("grp")
    z, p = dp // NP, dp % NP
    y, c = p // NC, p % NC
    count, width = emb_hbm.shape
    nchild = cent_hbm.shape[1]
    share = child_out.shape[0]
    scale = width ** (-0.5)

    def at_p(k):
        return (z * NP + (p + k) % NP, x)

    def at_z(to):
        return (to * NP + p, x)

    def at_x(k):
        return (dp, (x + k) % NX)

    def at_y(k):
        return (z * NP + ((y + k) % NY) * NC + c, x)

    other_core = (z * NP + y * NC + 1 - c, x)

    def signal(sem, device):
        pl.semaphore_signal(sem, inc=1, device_id=device, device_id_type=MESH)

    barrier = pltpu.get_barrier_semaphore()
    for k in range(1, NP):
        signal(barrier, at_p(k))
    for k in range(1, NX):
        signal(barrier, at_x(k))
    for k in range(1, NZ):
        signal(barrier, at_z((z + k) % NZ))

    loads = [
        pltpu.make_async_copy(ids_hbm, ids_ref, load_sem.at[0]),
        pltpu.make_async_copy(slot_hbm, slot_ref, load_sem.at[1]),
        pltpu.make_async_copy(emb_hbm, emb_ref, load_sem.at[2]),
        pltpu.make_async_copy(cc_hbm, cc_ref, load_sem.at[3]),
        pltpu.make_async_copy(cent_hbm, cent.at[:, pl.ds(0, nchild)], load_sem.at[4]),
    ]
    for load in loads:
        load.start()

    pending = []

    def send(src, dst, send_sem, recv_sem, device):
        copy = pltpu.make_async_remote_copy(
            src_ref=src, dst_ref=dst, send_sem=send_sem, recv_sem=recv_sem,
            device_id=device, device_id_type=MESH,
        )
        copy.start()
        return copy

    def keep(*args):
        pending.append(send(*args))

    def arrived(dst, sem):
        pltpu.make_async_remote_copy(
            src_ref=dst, dst_ref=dst, send_sem=sem, recv_sem=sem,
            device_id=at_x(1), device_id_type=MESH,
        ).wait_recv()

    for load in loads[:3]:
        load.wait()
    square = (count, count)
    diagonal = iota(square, 0) == iota(square, 1)
    ids_row = ids_ref[...]
    ids_col = jnp.sum(jnp.where(diagonal, ids_row, 0), axis=1, keepdims=True)
    slot_col = jnp.sum(jnp.where(diagonal, slot_ref[...], 0), axis=1, keepdims=True)
    placed = jnp.sum(jnp.where(ids_row == iota(square, 0), slot_col, 0), axis=0, keepdims=True)
    before = (ids_col == ids_row) & (iota(square, 0) < iota(square, 1))
    position = jnp.sum(before.astype(jnp.int32), axis=0, keepdims=True)
    target = placed * 2 + position

    emb = emb_ref[...]
    for j in range(4):
        r = iota((NP * 16, 1), 0)
        q = (r // 4) % 4
        d0, d1, d2, d3 = DISTANCE[4 * j : 4 * j + 4]
        distance = jnp.where(q == 0, d0, jnp.where(q == 1, d1, jnp.where(q == 2, d2, d3)))
        key = ((z + distance) % NZ) * (NP * 4) + (r // 16) * 4 + r % 4
        pick = (key == target).astype(jnp.float32)
        empty = jnp.sum(pick, axis=1, keepdims=True) < 0.5
        block = dot(pick.astype(jnp.bfloat16), emb)
        block = jnp.where(empty & (iota((1, width), 1) == 0), MARK, block)
        out_a[j] = block.astype(jnp.bfloat16).reshape(NP, 16, width)

    pl.semaphore_wait(barrier, NP - 1 + NX - 1 + NZ - 1)

    def stage_a(j):
        for k in range(1, NP):
            keep(out_a.at[j, (p + k) % NP], in_a.at[j, p], a_send.at[j, k], a_recv.at[j, k], at_p(k))
        in_a[j, p] = out_a[j, p]

    stage_a(0)
    stage_a(1)

    loads[3].wait()
    cc = cc_ref[...]
    cc32 = cc.astype(jnp.float32)
    coarse_norms = jnp.sum(cc32 * cc32, axis=1, keepdims=True)
    weights = column_softmax((dot_t(cc, emb) - 0.5 * coarse_norms) * scale).astype(jnp.bfloat16)
    cbuf[:, :, :, :width] = dot(weights, emb).reshape(NC, NY, 32, width)
    coarse_mass = jnp.sum(weights.astype(jnp.float32), axis=1, keepdims=True)
    cbuf[:, :, :, width:] = jnp.broadcast_to(coarse_mass, (count, 128)).reshape(NC, NY, 32, 128)
    keep(cbuf.at[1 - c], crecv, c_send, c_recv, other_core)
    own8 = (iota((8, count), 1) == c * 128 + y * 32 + x * 8 + iota((8, count), 0)).astype(jnp.bfloat16)
    rows8 = dot(own8, cc)
    for t in range(8):
        centers8[t] = rows8[:, 128 * t : 128 * (t + 1)]

    o, i = iota((128, 128), 0), iota((128, 128), 1)
    source = ((o // 2) % 8) * 16 + (o // 32) * 4 + ((o // 16) % 2) * 2 + o % 2
    reorder = (i == source).astype(jnp.bfloat16)

    def blocks_of(j):
        for k in range(1, NP):
            arrived(in_a.at[j, (p - k + NP) % NP], a_recv.at[j, k])
        blocks = dot(reorder, in_a[j].reshape(128, width)).astype(jnp.bfloat16)
        blocks = blocks.reshape(4, 2, 16, width)
        if j == 0:
            rows[0, 0] = blocks[0]
        zs[pl.ds(4 * j, 4)] = blocks

    def stage_z(n):
        keep(zs.at[n], rows.at[0, n], z_send.at[n], z_recv.at[n], at_z((z + DISTANCE[n]) % NZ))

    blocks_of(0)
    stage_a(2)

    def start_z(n):
        if n < NZ:
            if n % 4 == 0:
                blocks_of(n // 4)
                if n == 4:
                    stage_a(3)
            stage_z(n)

    for n in range(1, AHEAD[0] + 1):
        start_z(n)

    def coarse_step(s):
        if s == 0:
            arrived(crecv, c_recv)
            ybuf[...] = cbuf[c] + crecv[...]
            for k in range(1, NY):
                keep(ybuf.at[(y + k) % NY], yrecv.at[k], cy_send.at[k], cy_recv.at[k], at_y(k))
        if s == 1:
            total = ybuf[y]
            for k in range(1, NY):
                arrived(yrecv.at[k], cy_recv.at[k])
                total = total + yrecv[k]
            xbuf[...] = total.reshape(NX, 8, width + 128)
            for k in range(1, NX):
                keep(xbuf.at[(x + k) % NX], xrecv.at[k], cx_send.at[k], cx_recv.at[k], at_x(k))
        if s == 2:
            total = xbuf[x]
            for k in range(1, NX):
                arrived(xrecv.at[k], cx_recv.at[k])
                total = total + xrecv[k]
            for t in range(8):
                zbuf[t, 0] = total[:, 128 * t : 128 * (t + 1)]
                zbuf[t, 1] = total[:, width:]

                @pl.when(z == 2 * t)
                def _():
                    zrecv[z] = zbuf[t]

                @pl.when(z != 2 * t)
                def _():
                    send(zbuf.at[t], zrecv.at[z], cz_send.at[t], cz_recv.at[z], at_z(2 * t))
        if s == 3:

            @pl.when(z % 2 == 0)
            def _():
                for k in range(1, NZ):
                    arrived(zrecv.at[(z + k) % NZ], cz_recv.at[(z + k) % NZ])
                total = jnp.sum(zrecv[...], axis=0)
                tiles[z // 2] = (total[0] + prior_weight * centers8[z // 2]) / (total[1] + prior_weight)
                for k in range(1, NZ):
                    send(
                        tiles.at[z // 2], tiles.at[z // 2], gz_send.at[k], gz_recv.at[z // 2],
                        at_z((z + k) % NZ),
                    )
        if s == 4:
            for t in range(8):

                @pl.when(z != 2 * t)
                def _():
                    arrived(tiles.at[t], gz_recv.at[t])

            for t in range(8):
                coarse_out[c, y, x, :, pl.ds(128 * t, 128)] = tiles[t]
            for k in range(1, NX):
                keep(coarse_out.at[c, y, x], coarse_out.at[c, y, x], gx_send.at[k], gx_recv.at[k], at_x(k))
        if s == 5:
            for k in range(1, NX):
                arrived(coarse_out.at[c, y, (x - k + NX) % NX], gx_recv.at[k])
            for k in range(1, NY):
                keep(coarse_out.at[c, y], coarse_out.at[c, y], gy_send.at[k], gy_recv.at[k], at_y(k))
        if s == 6:
            for k in range(1, NY):
                arrived(coarse_out.at[c, (y - k + NY) % NY], gy_recv.at[k])
            keep(coarse_out.at[c], coarse_out.at[c], gc_send, gc_recv, other_core)
        if s == 7:
            arrived(coarse_out.at[1 - c], gc_recv)

    loads[4].wait()
    first = (iota((16, width), 0) == 0) & (iota((16, width), 1) == 0)
    for b in range(2):
        c32 = cent[b, :nchild].astype(jnp.float32)
        norms[b] = jnp.sum(c32 * c32, axis=1, keepdims=True)
        cent[b, nchild:] = first.astype(jnp.bfloat16)
    acc[...] = jnp.zeros_like(acc)
    mass[...] = jnp.zeros_like(mass)
    mine = (iota((128, nchild), 1) == iota((128, nchild), 0) + x * share) & (iota((128, nchild), 0) < share)
    mine = mine.astype(jnp.bfloat16)

    def score(j):
        def one(b, carry):
            block = rows[:, pl.ds(4 * j, 4), b].reshape(256, width)
            products = dot_t(cent[b], block)
            weights = column_softmax((products[:nchild] - 0.5 * norms[b]) * scale)
            weights = jnp.where(products[nchild : nchild + 1] < 0.5 * MARK, weights, 0.0)
            own = dot(mine, weights.astype(jnp.bfloat16))
            mass[b] += jnp.sum(own, axis=1, keepdims=True)
            acc[b] += dot(own.astype(jnp.bfloat16), block)
            return carry

        lax.fori_loop(0, 2, one, 0)

    def pass_on(n):
        if n > 0:
            arrived(rows.at[0, n], z_recv.at[n])
            for m in range(AHEAD[n - 1] + 1, AHEAD[n] + 1):
                start_z(m)
        keep(rows.at[0, n], rows.at[1, n], x_send.at[n, 0], x_recv.at[n, 0], at_x(1))
        keep(rows.at[0, n], rows.at[3, n], x_send.at[n, 1], x_recv.at[n, 1], at_x(3))

    def relay(n):
        arrived(rows.at[1, n], x_recv.at[n, 0])
        keep(rows.at[1, n, 0], rows.at[2, n, 0], r_send.at[n, 0], r_recv.at[n, 0], at_x(1))
        arrived(rows.at[3, n], x_recv.at[n, 1])
        keep(rows.at[3, n, 1], rows.at[2, n, 1], r_send.at[n, 1], r_recv.at[n, 1], at_x(3))

    def landed(n):
        arrived(rows.at[2, n, 0], r_recv.at[n, 0])
        arrived(rows.at[2, n, 1], r_recv.at[n, 1])

    steps = {1: 0, 3: 1, 5: 2, 11: 3, 14: 4, 16: 5, 17: 6}
    for n in range(NZ + 3):
        if n in steps:
            coarse_step(steps[n])
        if n < NZ:
            pass_on(n)
        if 1 <= n <= NZ:
            relay(n - 1)
        if 2 <= n < NZ + 2:
            landed(n - 2)
            if (n - 2) % 4 == 3:
                score((n - 2) // 4)
    for b in range(2):
        value = (acc[b] + prior_weight * dot(mine, cent[b, :nchild])) / (mass[b] + prior_weight)
        child_out[:, b] = value[:share]
    coarse_step(7)
    for copy in pending:
        copy.wait_send()
    def sent(src, sem):
        pltpu.make_async_remote_copy(
            src_ref=src, dst_ref=src, send_sem=sem, recv_sem=sem,
            device_id=at_x(1), device_id_type=MESH,
        ).wait_send()

    for t in range(8):

        @pl.when(z != 2 * t)
        def _():
            sent(zbuf.at[t], cz_send.at[t])

    @pl.when(z % 2 == 0)
    def _():
        for k in range(1, NZ):
            sent(tiles.at[z // 2], gz_send.at[k])


def on_device(embeddings, coarse_ids, owner_slot, coarse_centroids, child_centroids):
    count, width = embeddings.shape
    _, nchild, _ = child_centroids.shape
    share = nchild // NX
    f32, bf16 = jnp.float32, jnp.bfloat16
    vmem = pl.BlockSpec(memory_space=pltpu.VMEM)
    hbm = pl.BlockSpec(memory_space=pl.ANY)
    dma = pltpu.SemaphoreType.DMA
    wide = width + 128
    coarse, children = pl.pallas_call(
        kernel,
        out_shape=(
            jax.ShapeDtypeStruct((NC, NY, NX, 8, width), f32),
            jax.ShapeDtypeStruct((share, 2, width), f32),
        ),
        in_specs=[hbm] * 5,
        out_specs=(vmem, vmem),
        scratch_shapes=[
            pltpu.VMEM((1, count), jnp.int32),
            pltpu.VMEM((1, owner_slot.shape[0]), jnp.int32),
            pltpu.VMEM((count, width), bf16),
            pltpu.VMEM(coarse_centroids.shape, bf16),
            pltpu.VMEM((2, nchild + 16, width), bf16),
            pltpu.VMEM((2, nchild, 1), f32),
            pltpu.VMEM((2, 128, width), f32),
            pltpu.VMEM((2, 128, 1), f32),
            pltpu.VMEM((4, NP, 16, width), bf16),
            pltpu.VMEM((4, NP, 16, width), bf16),
            pltpu.VMEM((NZ, 2, 16, width), bf16),
            pltpu.VMEM((NX, NZ, 2, 16, width), bf16),
            pltpu.VMEM((NC, NY, 32, wide), f32),
            pltpu.VMEM((NY, 32, wide), f32),
            pltpu.VMEM((NY, 32, wide), f32),
            pltpu.VMEM((NY, 32, wide), f32),
            pltpu.VMEM((NX, 8, wide), f32),
            pltpu.VMEM((NX, 8, wide), f32),
            pltpu.VMEM((8, 2, 8, 128), f32),
            pltpu.VMEM((NZ, 2, 8, 128), f32),
            pltpu.VMEM((8, 8, 128), f32),
            pltpu.VMEM((8, 8, 128), f32),
            dma((5,)),
            dma((4, NP)), dma((4, NP)),
            dma((NZ,)), dma((NZ,)),
            dma((NZ, 2)), dma((NZ, 2)),
            dma((NZ, 2)), dma((NZ, 2)),
            dma, dma,
            dma((NY,)), dma((NY,)),
            dma((NX,)), dma((NX,)),
            dma((8,)), dma((NZ,)),
            dma((NZ,)), dma((8,)),
            dma((NX,)), dma((NX,)),
            dma((NY,)), dma((NY,)),
            dma, dma,
        ],
        compiler_params=pltpu.CompilerParams(
            collective_id=0, has_side_effects=True, vmem_limit_bytes=60 * 1024 * 1024
        ),
    )(
        coarse_ids.reshape(1, count),
        owner_slot.reshape(1, -1),
        embeddings,
        coarse_centroids,
        child_centroids,
    )
    return coarse.reshape(coarse_centroids.shape), children.transpose(1, 0, 2)


def solution(mesh):
    return jax.shard_map(
        on_device,
        mesh=mesh,
        in_specs=(P(("dp", "grp"), None), P(("dp", "grp"), None), P(), P(), P("dp", None, None)),
        out_specs=(P(), P("dp", "grp", None)),
        check_vma=False,
    )
```

```python
import jax
import jax.numpy as jnp
from jax import lax
from jax.experimental import pallas as pl
from jax.experimental.pallas import tpu as pltpu
from jax.sharding import PartitionSpec as P

MESH = pl.DeviceIdType.MESH
prior_weight = 1.0
NZ, NY, NC, NX = 16, 4, 2, 4
NP = NY * NC
MARK = 2.0**100
DISTANCE = (0, 1, 15, 2, 14, 3, 13, 4, 12, 5, 11, 6, 10, 7, 9, 8)
AHEAD = (8, 9, 10, 11, 12, 13, 14, 15, 15, 15, 15, 15, 15, 15, 15, 15)


def iota(shape, dim):
    return lax.broadcasted_iota(jnp.int32, shape, dim)


def dot(a, b):
    return jnp.dot(a, b, preferred_element_type=jnp.float32)


def dot_t(a, b):
    return lax.dot_general(a, b, (((1,), (1,)), ((), ())), preferred_element_type=jnp.float32)


def column_softmax(scores):
    raised = jnp.exp(scores - jnp.max(scores, axis=0, keepdims=True))
    return raised * (1.0 / jnp.sum(raised, axis=0, keepdims=True))


def kernel(
    ids_hbm, slot_hbm, emb_hbm, cc_hbm, cent_hbm,
    coarse_out, child_out,
    ids_ref, slot_ref, emb_ref, cc_ref, cent, norms, acc, mass, out_a, in_a, zs, rows,
    cbuf, crecv, ybuf, yrecv, xbuf, xrecv, zbuf, zrecv, tiles, centers8,
    load_sem, a_send, a_recv, z_send, z_recv, x_send, x_recv, r_send, r_recv,
    c_send, c_recv, cy_send, cy_recv, cx_send, cx_recv, cz_send, cz_recv,
    gz_send, gz_recv, gx_send, gx_recv, gy_send, gy_recv, gc_send, gc_recv,
):
    dp = lax.axis_index("dp")
    x = lax.axis_index("grp")
    z, p = dp // NP, dp % NP
    y, c = p // NC, p % NC
    count, width = emb_hbm.shape
    nchild = cent_hbm.shape[1]
    share = child_out.shape[0]
    scale = width ** (-0.5)

    def at_p(k):
        return (z * NP + (p + k) % NP, x)

    def at_z(to):
        return (to * NP + p, x)

    def at_x(k):
        return (dp, (x + k) % NX)

    def at_y(k):
        return (z * NP + ((y + k) % NY) * NC + c, x)

    other_core = (z * NP + y * NC + 1 - c, x)

    def signal(sem, device):
        pl.semaphore_signal(sem, inc=1, device_id=device, device_id_type=MESH)

    barrier = pltpu.get_barrier_semaphore()
    for k in range(1, NP):
        signal(barrier, at_p(k))
    for k in range(1, NX):
        signal(barrier, at_x(k))
    for k in range(1, NZ):
        signal(barrier, at_z((z + k) % NZ))

    loads = [
        pltpu.make_async_copy(ids_hbm, ids_ref, load_sem.at[0]),
        pltpu.make_async_copy(slot_hbm, slot_ref, load_sem.at[1]),
        pltpu.make_async_copy(emb_hbm, emb_ref, load_sem.at[2]),
        pltpu.make_async_copy(cc_hbm, cc_ref, load_sem.at[3]),
        pltpu.make_async_copy(cent_hbm, cent.at[:, pl.ds(0, nchild)], load_sem.at[4]),
    ]
    for load in loads:
        load.start()

    pending = []

    def send(src, dst, send_sem, recv_sem, device):
        copy = pltpu.make_async_remote_copy(
            src_ref=src, dst_ref=dst, send_sem=send_sem, recv_sem=recv_sem,
            device_id=device, device_id_type=MESH,
        )
        copy.start()
        return copy

    def keep(*args):
        pending.append(send(*args))

    def arrived(dst, sem):
        pltpu.make_async_remote_copy(
            src_ref=dst, dst_ref=dst, send_sem=sem, recv_sem=sem,
            device_id=at_x(1), device_id_type=MESH,
        ).wait_recv()

    for load in loads[:3]:
        load.wait()
    square = (count, count)
    diagonal = iota(square, 0) == iota(square, 1)
    ids_row = ids_ref[...]
    ids_col = jnp.sum(jnp.where(diagonal, ids_row, 0), axis=1, keepdims=True)
    slot_col = jnp.sum(jnp.where(diagonal, slot_ref[...], 0), axis=1, keepdims=True)
    placed = jnp.sum(jnp.where(ids_row == iota(square, 0), slot_col, 0), axis=0, keepdims=True)
    before = (ids_col == ids_row) & (iota(square, 0) < iota(square, 1))
    position = jnp.sum(before.astype(jnp.int32), axis=0, keepdims=True)
    target = placed * 2 + position

    emb = emb_ref[...]
    for j in range(4):
        r = iota((NP * 16, 1), 0)
        q = (r // 4) % 4
        d0, d1, d2, d3 = DISTANCE[4 * j : 4 * j + 4]
        distance = jnp.where(q == 0, d0, jnp.where(q == 1, d1, jnp.where(q == 2, d2, d3)))
        key = ((z + distance) % NZ) * (NP * 4) + (r // 16) * 4 + r % 4
        pick = (key == target).astype(jnp.float32)
        empty = jnp.sum(pick, axis=1, keepdims=True) < 0.5
        block = dot(pick.astype(jnp.bfloat16), emb)
        block = jnp.where(empty & (iota((1, width), 1) == 0), MARK, block)
        out_a[j] = block.astype(jnp.bfloat16).reshape(NP, 16, width)

    pl.semaphore_wait(barrier, NP - 1 + NX - 1 + NZ - 1)

    def stage_a(j):
        for k in range(1, NP):
            keep(out_a.at[j, (p + k) % NP], in_a.at[j, p], a_send.at[j, k], a_recv.at[j, k], at_p(k))
        in_a[j, p] = out_a[j, p]

    stage_a(0)
    stage_a(1)

    loads[3].wait()
    cc = cc_ref[...]
    cc32 = cc.astype(jnp.float32)
    coarse_norms = jnp.sum(cc32 * cc32, axis=1, keepdims=True)
    weights = column_softmax((dot_t(cc, emb) - 0.5 * coarse_norms) * scale).astype(jnp.bfloat16)
    cbuf[:, :, :, :width] = dot(weights, emb).reshape(NC, NY, 32, width)
    coarse_mass = jnp.sum(weights.astype(jnp.float32), axis=1, keepdims=True)
    cbuf[:, :, :, width:] = jnp.broadcast_to(coarse_mass, (count, 128)).reshape(NC, NY, 32, 128)
    keep(cbuf.at[1 - c], crecv, c_send, c_recv, other_core)
    own8 = (iota((8, count), 1) == c * 128 + y * 32 + x * 8 + iota((8, count), 0)).astype(jnp.bfloat16)
    rows8 = dot(own8, cc)
    for t in range(8):
        centers8[t] = rows8[:, 128 * t : 128 * (t + 1)]

    o, i = iota((128, 128), 0), iota((128, 128), 1)
    source = ((o // 2) % 8) * 16 + (o // 32) * 4 + ((o // 16) % 2) * 2 + o % 2
    reorder = (i == source).astype(jnp.bfloat16)

    def blocks_of(j):
        for k in range(1, NP):
            arrived(in_a.at[j, (p - k + NP) % NP], a_recv.at[j, k])
        blocks = dot(reorder, in_a[j].reshape(128, width)).astype(jnp.bfloat16)
        blocks = blocks.reshape(4, 2, 16, width)
        if j == 0:
            rows[0, 0] = blocks[0]
        zs[pl.ds(4 * j, 4)] = blocks

    def stage_z(n):
        keep(zs.at[n], rows.at[0, n], z_send.at[n], z_recv.at[n], at_z((z + DISTANCE[n]) % NZ))

    blocks_of(0)
    stage_a(2)

    def start_z(n):
        if n < NZ:
            if n % 4 == 0:
                blocks_of(n // 4)
                if n == 4:
                    stage_a(3)
            stage_z(n)

    for n in range(1, AHEAD[0] + 1):
        start_z(n)

    def coarse_step(s):
        if s == 0:
            arrived(crecv, c_recv)
            ybuf[...] = cbuf[c] + crecv[...]
            for k in range(1, NY):
                keep(ybuf.at[(y + k) % NY], yrecv.at[k], cy_send.at[k], cy_recv.at[k], at_y(k))
        if s == 1:
            total = ybuf[y]
            for k in range(1, NY):
                arrived(yrecv.at[k], cy_recv.at[k])
                total = total + yrecv[k]
            xbuf[...] = total.reshape(NX, 8, width + 128)
            for k in range(1, NX):
                keep(xbuf.at[(x + k) % NX], xrecv.at[k], cx_send.at[k], cx_recv.at[k], at_x(k))
        if s == 2:
            total = xbuf[x]
            for k in range(1, NX):
                arrived(xrecv.at[k], cx_recv.at[k])
                total = total + xrecv[k]
            for t in range(8):
                zbuf[t, 0] = total[:, 128 * t : 128 * (t + 1)]
                zbuf[t, 1] = total[:, width:]

                @pl.when(z == 2 * t)
                def _():
                    zrecv[z] = zbuf[t]

                @pl.when(z != 2 * t)
                def _():
                    send(zbuf.at[t], zrecv.at[z], cz_send.at[t], cz_recv.at[z], at_z(2 * t))
        if s == 3:

            @pl.when(z % 2 == 0)
            def _():
                for k in range(1, NZ):
                    arrived(zrecv.at[(z + k) % NZ], cz_recv.at[(z + k) % NZ])
                total = jnp.sum(zrecv[...], axis=0)
                tiles[z // 2] = (total[0] + prior_weight * centers8[z // 2]) / (total[1] + prior_weight)
                for k in range(1, NZ):
                    send(
                        tiles.at[z // 2], tiles.at[z // 2], gz_send.at[k], gz_recv.at[z // 2],
                        at_z((z + k) % NZ),
                    )
        if s == 4:
            for t in range(8):

                @pl.when(z != 2 * t)
                def _():
                    arrived(tiles.at[t], gz_recv.at[t])

            for t in range(8):
                coarse_out[c, y, x, :, pl.ds(128 * t, 128)] = tiles[t]
            for k in range(1, NX):
                keep(coarse_out.at[c, y, x], coarse_out.at[c, y, x], gx_send.at[k], gx_recv.at[k], at_x(k))
        if s == 5:
            for k in range(1, NX):
                arrived(coarse_out.at[c, y, (x - k + NX) % NX], gx_recv.at[k])
            for k in range(1, NY):
                keep(coarse_out.at[c, y], coarse_out.at[c, y], gy_send.at[k], gy_recv.at[k], at_y(k))
            to_core(0)
        if s == 6:
            for k in range(1, NY):
                arrived(coarse_out.at[c, (y - k + NY) % NY], gy_recv.at[k])
                to_core(k)
        if s == 7:
            for k in range(NY):
                arrived(coarse_out.at[1 - c, (y - k + NY) % NY], gc_recv.at[k])

    def to_core(k):
        part = coarse_out.at[c, (y - k + NY) % NY]
        keep(part, part, gc_send.at[k], gc_recv.at[k], other_core)

    loads[4].wait()
    first = (iota((16, width), 0) == 0) & (iota((16, width), 1) == 0)
    for b in range(2):
        c32 = cent[b, :nchild].astype(jnp.float32)
        norms[b] = jnp.sum(c32 * c32, axis=1, keepdims=True)
        cent[b, nchild:] = first.astype(jnp.bfloat16)
    acc[...] = jnp.zeros_like(acc)
    mass[...] = jnp.zeros_like(mass)
    mine = (iota((128, nchild), 1) == iota((128, nchild), 0) + x * share) & (iota((128, nchild), 0) < share)
    mine = mine.astype(jnp.bfloat16)

    def score(j):
        def one(b, carry):
            block = rows[:, pl.ds(4 * j, 4), b].reshape(256, width)
            products = dot_t(cent[b], block)
            weights = column_softmax((products[:nchild] - 0.5 * norms[b]) * scale)
            weights = jnp.where(products[nchild : nchild + 1] < 0.5 * MARK, weights, 0.0)
            own = dot(mine, weights.astype(jnp.bfloat16))
            mass[b] += jnp.sum(own, axis=1, keepdims=True)
            acc[b] += dot(own.astype(jnp.bfloat16), block)
            return carry

        lax.fori_loop(0, 2, one, 0)

    def pass_on(n):
        if n > 0:
            arrived(rows.at[0, n], z_recv.at[n])
            for m in range(AHEAD[n - 1] + 1, AHEAD[n] + 1):
                start_z(m)
        keep(rows.at[0, n], rows.at[1, n], x_send.at[n, 0], x_recv.at[n, 0], at_x(1))
        keep(rows.at[0, n], rows.at[3, n], x_send.at[n, 1], x_recv.at[n, 1], at_x(3))

    def relay(n):
        arrived(rows.at[1, n], x_recv.at[n, 0])
        keep(rows.at[1, n, 0], rows.at[2, n, 0], r_send.at[n, 0], r_recv.at[n, 0], at_x(1))
        arrived(rows.at[3, n], x_recv.at[n, 1])
        keep(rows.at[3, n, 1], rows.at[2, n, 1], r_send.at[n, 1], r_recv.at[n, 1], at_x(3))

    def landed(n):
        arrived(rows.at[2, n, 0], r_recv.at[n, 0])
        arrived(rows.at[2, n, 1], r_recv.at[n, 1])

    steps = {0: 0, 2: 1, 3: 2, 10: 3, 13: 4, 15: 5, 17: 6}
    for n in range(NZ + 3):
        if n in steps:
            coarse_step(steps[n])
        if n < NZ:
            pass_on(n)
        if 1 <= n <= NZ:
            relay(n - 1)
        if 2 <= n < NZ + 2:
            landed(n - 2)
            if (n - 2) % 4 == 3:
                score((n - 2) // 4)
    for b in range(2):
        value = (acc[b] + prior_weight * dot(mine, cent[b, :nchild])) / (mass[b] + prior_weight)
        child_out[:, b] = value[:share]
    coarse_step(7)
    for copy in pending:
        copy.wait_send()
    def sent(src, sem):
        pltpu.make_async_remote_copy(
            src_ref=src, dst_ref=src, send_sem=sem, recv_sem=sem,
            device_id=at_x(1), device_id_type=MESH,
        ).wait_send()

    for t in range(8):

        @pl.when(z != 2 * t)
        def _():
            sent(zbuf.at[t], cz_send.at[t])

    @pl.when(z % 2 == 0)
    def _():
        for k in range(1, NZ):
            sent(tiles.at[z // 2], gz_send.at[k])


def on_device(embeddings, coarse_ids, owner_slot, coarse_centroids, child_centroids):
    count, width = embeddings.shape
    _, nchild, _ = child_centroids.shape
    share = nchild // NX
    f32, bf16 = jnp.float32, jnp.bfloat16
    vmem = pl.BlockSpec(memory_space=pltpu.VMEM)
    hbm = pl.BlockSpec(memory_space=pl.ANY)
    dma = pltpu.SemaphoreType.DMA
    wide = width + 128
    coarse, children = pl.pallas_call(
        kernel,
        out_shape=(
            pltpu.VMEM((NC, NY, NX, 8, width), f32),
            pltpu.VMEM((share, 2, width), f32),
        ),
        in_specs=[hbm] * 5,
        out_specs=(vmem, vmem),
        scratch_shapes=[
            pltpu.VMEM((1, count), jnp.int32),
            pltpu.VMEM((1, owner_slot.shape[0]), jnp.int32),
            pltpu.VMEM((count, width), bf16),
            pltpu.VMEM(coarse_centroids.shape, bf16),
            pltpu.VMEM((2, nchild + 16, width), bf16),
            pltpu.VMEM((2, nchild, 1), f32),
            pltpu.VMEM((2, 128, width), f32),
            pltpu.VMEM((2, 128, 1), f32),
            pltpu.VMEM((4, NP, 16, width), bf16),
            pltpu.VMEM((4, NP, 16, width), bf16),
            pltpu.VMEM((NZ, 2, 16, width), bf16),
            pltpu.VMEM((NX, NZ, 2, 16, width), bf16),
            pltpu.VMEM((NC, NY, 32, wide), f32),
            pltpu.VMEM((NY, 32, wide), f32),
            pltpu.VMEM((NY, 32, wide), f32),
            pltpu.VMEM((NY, 32, wide), f32),
            pltpu.VMEM((NX, 8, wide), f32),
            pltpu.VMEM((NX, 8, wide), f32),
            pltpu.VMEM((8, 2, 8, 128), f32),
            pltpu.VMEM((NZ, 2, 8, 128), f32),
            pltpu.VMEM((8, 8, 128), f32),
            pltpu.VMEM((8, 8, 128), f32),
            dma((5,)),
            dma((4, NP)), dma((4, NP)),
            dma((NZ,)), dma((NZ,)),
            dma((NZ, 2)), dma((NZ, 2)),
            dma((NZ, 2)), dma((NZ, 2)),
            dma, dma,
            dma((NY,)), dma((NY,)),
            dma((NX,)), dma((NX,)),
            dma((8,)), dma((NZ,)),
            dma((NZ,)), dma((8,)),
            dma((NX,)), dma((NX,)),
            dma((NY,)), dma((NY,)),
            dma((NY,)), dma((NY,)),
        ],
        compiler_params=pltpu.CompilerParams(
            collective_id=0, has_side_effects=True, vmem_limit_bytes=60 * 1024 * 1024
        ),
    )(
        coarse_ids.reshape(1, count),
        owner_slot.reshape(1, -1),
        embeddings,
        coarse_centroids,
        child_centroids,
    )
    return coarse.reshape(coarse_centroids.shape), children.transpose(1, 0, 2)


def solution(mesh):
    return jax.shard_map(
        on_device,
        mesh=mesh,
        in_specs=(P(("dp", "grp"), None), P(("dp", "grp"), None), P(), P(), P("dp", None, None)),
        out_specs=(P(), P("dp", "grp", None)),
        check_vma=False,
    )
```

```python
import jax
import jax.numpy as jnp
from jax import lax
from jax.experimental import pallas as pl
from jax.experimental.pallas import tpu as pltpu
from jax.sharding import PartitionSpec as P

MESH = pl.DeviceIdType.MESH
prior_weight = 1.0
NZ, NY, NC, NX = 16, 4, 2, 4
NP = NY * NC
MARK = 2.0**100
DISTANCE = (0, 1, 15, 2, 14, 3, 13, 4, 12, 5, 11, 6, 10, 7, 9, 8)
AHEAD = (8, 9, 10, 11, 12, 13, 14, 15, 15, 15, 15, 15, 15, 15, 15, 15)


def iota(shape, dim):
    return lax.broadcasted_iota(jnp.int32, shape, dim)


def dot(a, b):
    return jnp.dot(a, b, preferred_element_type=jnp.float32)


def dot_t(a, b):
    return lax.dot_general(a, b, (((1,), (1,)), ((), ())), preferred_element_type=jnp.float32)


def column_softmax(scores):
    raised = jnp.exp(scores - jnp.max(scores, axis=0, keepdims=True))
    return raised * (1.0 / jnp.sum(raised, axis=0, keepdims=True))


def kernel(
    ids_hbm, slot_hbm, emb_hbm, cc_hbm, cent_hbm,
    coarse_out, child_out,
    ids_ref, slot_ref, emb_ref, cc_ref, cent, norms, acc, mass, out_a, in_a, zs, rows,
    cbuf, crecv, ybuf, yrecv, xbuf, xrecv, zbuf, zrecv, tiles, centers8,
    load_sem, a_send, a_recv, z_send, z_recv, x_send, x_recv, r_send, r_recv,
    c_send, c_recv, cy_send, cy_recv, cx_send, cx_recv, cz_send, cz_recv,
    gz_send, gz_recv, gx_send, gx_recv, gy_send, gy_recv, gc_send, gc_recv,
):
    dp = lax.axis_index("dp")
    x = lax.axis_index("grp")
    z, p = dp // NP, dp % NP
    y, c = p // NC, p % NC
    count, width = emb_hbm.shape
    nchild = cent_hbm.shape[1]
    share = child_out.shape[0]
    scale = width ** (-0.5)

    def at_p(k):
        return (z * NP + (p + k) % NP, x)

    def at_z(to):
        return (to * NP + p, x)

    def at_x(k):
        return (dp, (x + k) % NX)

    def at_y(k):
        return (z * NP + ((y + k) % NY) * NC + c, x)

    other_core = (z * NP + y * NC + 1 - c, x)

    def signal(sem, device):
        pl.semaphore_signal(sem, inc=1, device_id=device, device_id_type=MESH)

    barrier = pltpu.get_barrier_semaphore()
    for k in range(1, NP):
        signal(barrier, at_p(k))
    for k in range(1, NX):
        signal(barrier, at_x(k))
    for k in range(1, NZ):
        signal(barrier, at_z((z + k) % NZ))

    loads = [
        pltpu.make_async_copy(ids_hbm, ids_ref, load_sem.at[0]),
        pltpu.make_async_copy(slot_hbm, slot_ref, load_sem.at[1]),
        pltpu.make_async_copy(emb_hbm, emb_ref, load_sem.at[2]),
        pltpu.make_async_copy(cc_hbm, cc_ref, load_sem.at[3]),
        pltpu.make_async_copy(cent_hbm, cent.at[:, pl.ds(0, nchild)], load_sem.at[4]),
    ]
    for load in loads:
        load.start()

    pending, along_z = [], []

    def send(src, dst, send_sem, recv_sem, device):
        copy = pltpu.make_async_remote_copy(
            src_ref=src, dst_ref=dst, send_sem=send_sem, recv_sem=recv_sem,
            device_id=device, device_id_type=MESH,
        )
        copy.start()
        return copy

    def keep(*args):
        pending.append(send(*args))

    def arrived(dst, sem):
        pltpu.make_async_remote_copy(
            src_ref=dst, dst_ref=dst, send_sem=sem, recv_sem=sem,
            device_id=at_x(1), device_id_type=MESH,
        ).wait_recv()

    for load in loads[:3]:
        load.wait()
    square = (count, count)
    diagonal = iota(square, 0) == iota(square, 1)
    ids_row = ids_ref[...]
    ids_col = jnp.sum(jnp.where(diagonal, ids_row, 0), axis=1, keepdims=True)
    slot_col = jnp.sum(jnp.where(diagonal, slot_ref[...], 0), axis=1, keepdims=True)
    placed = jnp.sum(jnp.where(ids_row == iota(square, 0), slot_col, 0), axis=0, keepdims=True)
    before = (ids_col == ids_row) & (iota(square, 0) < iota(square, 1))
    position = jnp.sum(before.astype(jnp.int32), axis=0, keepdims=True)
    target = placed * 2 + position

    emb = emb_ref[...]
    for j in range(4):
        r = iota((NP * 16, 1), 0)
        q = (r // 4) % 4
        d0, d1, d2, d3 = DISTANCE[4 * j : 4 * j + 4]
        distance = jnp.where(q == 0, d0, jnp.where(q == 1, d1, jnp.where(q == 2, d2, d3)))
        key = ((z + distance) % NZ) * (NP * 4) + (r // 16) * 4 + r % 4
        pick = (key == target).astype(jnp.float32)
        empty = jnp.sum(pick, axis=1, keepdims=True) < 0.5
        block = dot(pick.astype(jnp.bfloat16), emb)
        block = jnp.where(empty & (iota((1, width), 1) == 0), MARK, block)
        out_a[j] = block.astype(jnp.bfloat16).reshape(NP, 16, width)

    pl.semaphore_wait(barrier, NP - 1 + NX - 1 + NZ - 1)

    def stage_a(j):
        for k in range(1, NP):
            keep(out_a.at[j, (p + k) % NP], in_a.at[j, p], a_send.at[j, k], a_recv.at[j, k], at_p(k))
        in_a[j, p] = out_a[j, p]

    stage_a(0)
    stage_a(1)

    loads[3].wait()
    cc = cc_ref[...]
    cc32 = cc.astype(jnp.float32)
    coarse_norms = jnp.sum(cc32 * cc32, axis=1, keepdims=True)
    weights = column_softmax((dot_t(cc, emb) - 0.5 * coarse_norms) * scale).astype(jnp.bfloat16)
    cbuf[:, :, :, :width] = dot(weights, emb).reshape(NC, NY, 32, width)
    coarse_mass = jnp.sum(weights.astype(jnp.float32), axis=1, keepdims=True)
    cbuf[:, :, :, width:] = jnp.broadcast_to(coarse_mass, (count, 128)).reshape(NC, NY, 32, 128)
    keep(cbuf.at[1 - c], crecv, c_send, c_recv, other_core)
    own8 = (iota((8, count), 1) == c * 128 + y * 32 + x * 8 + iota((8, count), 0)).astype(jnp.bfloat16)
    rows8 = dot(own8, cc)
    for t in range(8):
        centers8[t] = rows8[:, 128 * t : 128 * (t + 1)]

    o, i = iota((128, 128), 0), iota((128, 128), 1)
    source = ((o // 2) % 8) * 16 + (o // 32) * 4 + ((o // 16) % 2) * 2 + o % 2
    reorder = (i == source).astype(jnp.bfloat16)

    def blocks_of(j):
        for k in range(1, NP):
            arrived(in_a.at[j, (p - k + NP) % NP], a_recv.at[j, k])
        blocks = dot(reorder, in_a[j].reshape(128, width)).astype(jnp.bfloat16)
        blocks = blocks.reshape(4, 2, 16, width)
        if j == 0:
            rows[0, 0] = blocks[0]
        zs[pl.ds(4 * j, 4)] = blocks

    def stage_z(n):
        copy = send(zs.at[n], rows.at[0, n], z_send.at[n], z_recv.at[n], at_z((z + DISTANCE[n]) % NZ))
        along_z.append(copy)

    blocks_of(0)
    stage_a(2)

    def start_z(n):
        if n < NZ:
            if n % 4 == 0:
                blocks_of(n // 4)
                if n == 4:
                    stage_a(3)
            stage_z(n)

    for n in range(1, AHEAD[0] + 1):
        start_z(n)

    def coarse_step(s):
        if s == 0:
            arrived(crecv, c_recv)
            ybuf[...] = cbuf[c] + crecv[...]
            for k in range(1, NY):
                keep(ybuf.at[(y + k) % NY], yrecv.at[k], cy_send.at[k], cy_recv.at[k], at_y(k))
        if s == 1:
            total = ybuf[y]
            for k in range(1, NY):
                arrived(yrecv.at[k], cy_recv.at[k])
                total = total + yrecv[k]
            xbuf[...] = total.reshape(NX, 8, width + 128)
            for k in range(1, NX):
                keep(xbuf.at[(x + k) % NX], xrecv.at[k], cx_send.at[k], cx_recv.at[k], at_x(k))
        if s == 2:
            total = xbuf[x]
            for k in range(1, NX):
                arrived(xrecv.at[k], cx_recv.at[k])
                total = total + xrecv[k]
            for t in range(8):
                zbuf[t, 0] = total[:, 128 * t : 128 * (t + 1)]
                zbuf[t, 1] = total[:, width:]

                @pl.when(z == 2 * t)
                def _():
                    zrecv[z] = zbuf[t]

                @pl.when(z != 2 * t)
                def _():
                    send(zbuf.at[t], zrecv.at[z], cz_send.at[t], cz_recv.at[z], at_z(2 * t))
        if s == 3:

            @pl.when(z % 2 == 0)
            def _():
                for k in range(1, NZ):
                    arrived(zrecv.at[(z + k) % NZ], cz_recv.at[(z + k) % NZ])
                total = jnp.sum(zrecv[...], axis=0)
                tiles[z // 2] = (total[0] + prior_weight * centers8[z // 2]) / (total[1] + prior_weight)
                for k in range(1, NZ):
                    send(
                        tiles.at[z // 2], tiles.at[z // 2], gz_send.at[k], gz_recv.at[z // 2],
                        at_z((z + k) % NZ),
                    )
        if s == 4:
            for t in range(8):

                @pl.when(z != 2 * t)
                def _():
                    arrived(tiles.at[t], gz_recv.at[t])

            for t in range(8):
                coarse_out[c, y, x, :, pl.ds(128 * t, 128)] = tiles[t]
            for k in range(1, NX):
                keep(coarse_out.at[c, y, x], coarse_out.at[c, y, x], gx_send.at[k], gx_recv.at[k], at_x(k))
        if s == 5:
            for k in range(1, NX):
                arrived(coarse_out.at[c, y, (x - k + NX) % NX], gx_recv.at[k])
            for k in range(1, NY):
                keep(coarse_out.at[c, y], coarse_out.at[c, y], gy_send.at[k], gy_recv.at[k], at_y(k))
            to_core(0)
        if s == 6:
            for k in range(1, NY):
                arrived(coarse_out.at[c, (y - k + NY) % NY], gy_recv.at[k])
                to_core(k)
        if s == 7:
            for k in range(NY):
                arrived(coarse_out.at[1 - c, (y - k + NY) % NY], gc_recv.at[k])

    def to_core(k):
        part = coarse_out.at[c, (y - k + NY) % NY]
        keep(part, part, gc_send.at[k], gc_recv.at[k], other_core)

    loads[4].wait()
    first = (iota((16, width), 0) == 0) & (iota((16, width), 1) == 0)
    for b in range(2):
        c32 = cent[b, :nchild].astype(jnp.float32)
        norms[b] = jnp.sum(c32 * c32, axis=1, keepdims=True)
        cent[b, nchild:] = first.astype(jnp.bfloat16)
    acc[...] = jnp.zeros_like(acc)
    mass[...] = jnp.zeros_like(mass)
    mine = (iota((128, nchild), 1) == iota((128, nchild), 0) + x * share) & (iota((128, nchild), 0) < share)
    mine = mine.astype(jnp.bfloat16)

    def score(j):
        def one(b, carry):
            block = rows[:, pl.ds(4 * j, 4), b].reshape(256, width)
            products = dot_t(cent[b], block)
            weights = column_softmax((products[:nchild] - 0.5 * norms[b]) * scale)
            weights = jnp.where(products[nchild : nchild + 1] < 0.5 * MARK, weights, 0.0)
            own = dot(mine, weights.astype(jnp.bfloat16))
            mass[b] += jnp.sum(own, axis=1, keepdims=True)
            acc[b] += dot(own.astype(jnp.bfloat16), block)
            return carry

        lax.fori_loop(0, 2, one, 0)

    def pass_on(n):
        if n > 0:
            arrived(rows.at[0, n], z_recv.at[n])
            for m in range(AHEAD[n - 1] + 1, AHEAD[n] + 1):
                start_z(m)
        keep(rows.at[0, n], rows.at[1, n], x_send.at[n, 0], x_recv.at[n, 0], at_x(1))
        keep(rows.at[0, n], rows.at[3, n], x_send.at[n, 1], x_recv.at[n, 1], at_x(3))

    def relay(n):
        arrived(rows.at[1, n], x_recv.at[n, 0])
        keep(rows.at[1, n, 0], rows.at[2, n, 0], r_send.at[n, 0], r_recv.at[n, 0], at_x(1))
        arrived(rows.at[3, n], x_recv.at[n, 1])
        keep(rows.at[3, n, 1], rows.at[2, n, 1], r_send.at[n, 1], r_recv.at[n, 1], at_x(3))

    def landed(n):
        arrived(rows.at[2, n, 0], r_recv.at[n, 0])
        arrived(rows.at[2, n, 1], r_recv.at[n, 1])

    steps = {0: 0, 2: 1, 3: 2, 10: 3, 13: 4, 15: 5, 17: 6}
    started, done = [], 0
    for n in range(NZ + 3):
        if n in steps:
            coarse_step(steps[n])
        if n < NZ:
            pass_on(n)
        if 1 <= n <= NZ:
            relay(n - 1)
        if 2 <= n < NZ + 2:
            landed(n - 2)
            if (n - 2) % 4 == 3:
                score((n - 2) // 4)
        started.append(len(pending))
        if n >= 4:
            for copy in pending[done : started[n - 4]]:
                copy.wait_send()
            done = started[n - 4]
    for b in range(2):
        value = (acc[b] + prior_weight * dot(mine, cent[b, :nchild])) / (mass[b] + prior_weight)
        child_out[:, b] = value[:share]
    coarse_step(7)
    for copy in pending[done:] + along_z:
        copy.wait_send()
    def sent(src, sem):
        pltpu.make_async_remote_copy(
            src_ref=src, dst_ref=src, send_sem=sem, recv_sem=sem,
            device_id=at_x(1), device_id_type=MESH,
        ).wait_send()

    for t in range(8):

        @pl.when(z != 2 * t)
        def _():
            sent(zbuf.at[t], cz_send.at[t])

    @pl.when(z % 2 == 0)
    def _():
        for k in range(1, NZ):
            sent(tiles.at[z // 2], gz_send.at[k])


def on_device(embeddings, coarse_ids, owner_slot, coarse_centroids, child_centroids):
    count, width = embeddings.shape
    _, nchild, _ = child_centroids.shape
    share = nchild // NX
    f32, bf16 = jnp.float32, jnp.bfloat16
    vmem = pl.BlockSpec(memory_space=pltpu.VMEM)
    hbm = pl.BlockSpec(memory_space=pl.ANY)
    dma = pltpu.SemaphoreType.DMA
    wide = width + 128
    coarse, children = pl.pallas_call(
        kernel,
        out_shape=(
            pltpu.VMEM((NC, NY, NX, 8, width), f32),
            pltpu.VMEM((share, 2, width), f32),
        ),
        in_specs=[hbm] * 5,
        out_specs=(vmem, vmem),
        scratch_shapes=[
            pltpu.VMEM((1, count), jnp.int32),
            pltpu.VMEM((1, owner_slot.shape[0]), jnp.int32),
            pltpu.VMEM((count, width), bf16),
            pltpu.VMEM(coarse_centroids.shape, bf16),
            pltpu.VMEM((2, nchild + 16, width), bf16),
            pltpu.VMEM((2, nchild, 1), f32),
            pltpu.VMEM((2, 128, width), f32),
            pltpu.VMEM((2, 128, 1), f32),
            pltpu.VMEM((4, NP, 16, width), bf16),
            pltpu.VMEM((4, NP, 16, width), bf16),
            pltpu.VMEM((NZ, 2, 16, width), bf16),
            pltpu.VMEM((NX, NZ, 2, 16, width), bf16),
            pltpu.VMEM((NC, NY, 32, wide), f32),
            pltpu.VMEM((NY, 32, wide), f32),
            pltpu.VMEM((NY, 32, wide), f32),
            pltpu.VMEM((NY, 32, wide), f32),
            pltpu.VMEM((NX, 8, wide), f32),
            pltpu.VMEM((NX, 8, wide), f32),
            pltpu.VMEM((8, 2, 8, 128), f32),
            pltpu.VMEM((NZ, 2, 8, 128), f32),
            pltpu.VMEM((8, 8, 128), f32),
            pltpu.VMEM((8, 8, 128), f32),
            dma((5,)),
            dma((4, NP)), dma((4, NP)),
            dma((NZ,)), dma((NZ,)),
            dma((NZ, 2)), dma((NZ, 2)),
            dma((NZ, 2)), dma((NZ, 2)),
            dma, dma,
            dma((NY,)), dma((NY,)),
            dma((NX,)), dma((NX,)),
            dma((8,)), dma((NZ,)),
            dma((NZ,)), dma((8,)),
            dma((NX,)), dma((NX,)),
            dma((NY,)), dma((NY,)),
            dma((NY,)), dma((NY,)),
        ],
        compiler_params=pltpu.CompilerParams(
            collective_id=0, has_side_effects=True, vmem_limit_bytes=60 * 1024 * 1024
        ),
    )(
        coarse_ids.reshape(1, count),
        owner_slot.reshape(1, -1),
        embeddings,
        coarse_centroids,
        child_centroids,
    )
    return coarse.reshape(coarse_centroids.shape), children.transpose(1, 0, 2)


def solution(mesh):
    return jax.shard_map(
        on_device,
        mesh=mesh,
        in_specs=(P(("dp", "grp"), None), P(("dp", "grp"), None), P(), P(), P("dp", None, None)),
        out_specs=(P(), P("dp", "grp", None)),
        check_vma=False,
    )
```
